512 devices in a mesh: tm: 64 (over y_hi, z, core), lat: 8 (over x, y_lo).
Axes of the slice: x: 4, y: 8 (y_hi: 4, y_lo: 2; y = y_hi * 2 + y_lo), z: 8, core: 2. Of those that a mesh axis runs over, the one named last changes fastest.
Arguments:
- states: float32 [64, 3, 512, 256], P('tm', None, 'lat'), may hold values from -0.75 to 0.75
- initial_state: float32 [3, 512, 256], P(None, 'lat'), may hold values from -0.75 to 0.75
- coarse_decay: float32 [512, 256], P('lat'), may hold values from 0.015625 to 2
Outputs:
- corrected: float32 [64, 3, 512, 256], P('tm', None, 'lat')
- residual: float32 [64, 3, 512, 256], P('tm', None, 'lat')
The draws below stay inside these ranges and needn't reach their ends.
All inputs are finite; a program needn't handle non-finite values.
Results may differ from the reference program's by a relative error of at most 0.000028.
Values sent between devices are 32-bit elements; how exact they have to be, the bound alone decides.
No kernel may reach another device: no remote copies, remote signals or barrier semaphores. Data moves between devices by JAX's collectives and lax.ppermute only.
A program may use at most 128 MiB of HBM per device.

```python
import math
import jax
import jax.numpy as jnp
from jax import lax

NLAT = 512
NLON = 256
STEPS = 4
BLOCKS = 64


def steps_of(key, shape, cuts, smallest, high):
    def one(axis_at, shards_of):
        heights = jax.random.uniform(jax.random.fold_in(jax.random.fold_in(key, 6), axis_at), (shards_of,), jnp.float32, smallest / len(cuts), high / len(cuts))
        return jnp.repeat(jnp.exp(heights), shape[axis_at] // shards_of).reshape((-1,) + (1,) * (len(shape) - axis_at - 1))

    factor_of = one(*cuts[0])
    for cut in cuts[1:]:
        factor_of = factor_of * one(*cut)
    return factor_of


def normal_values(rng, dims, width, most, shards=(), kind=jnp.bfloat16):
    gain = steps_of(rng, dims, shards, -0.22, 0.18) if shards else 1.0
    values = jax.random.normal(rng, dims, jnp.float32) * width * gain
    return jnp.minimum(jnp.maximum(values, -most), most).astype(kind)


def setup_inputs(seed: int = 0) -> dict:
    key_of = jax.random.split(jax.random.key(seed), 4)
    return {
        "states": normal_values(key_of[0], (BLOCKS, 3, NLAT, NLON), 0.25, 0.75, ((0, 64), (2, 8)), jnp.float32),
        "initial_state": normal_values(key_of[1], (3, NLAT, NLON), 0.25, 0.75, ((1, 8),), jnp.float32),
        "coarse_decay": jnp.clip(jnp.exp(math.log(2.0) - 4.8520303 * jax.random.uniform(key_of[2], (NLAT, NLON), jnp.float32) ** steps_of(key_of[2], (NLAT, NLON), ((0, 8),), -0.2, 0.2)), 0.015625, 2.0),
    }


TIME_STEP = 0.25
GRAVITY = 1.0
CORIOLIS = 0.3
MEAN_DEPTH = 1.0
TURN_ANGLE = 1.2


def tendency(middle, upper, lower):
    east_side = jnp.roll(middle, -1, axis=2)
    west_side = jnp.roll(middle, 1, axis=2)
    average = (east_side + west_side + upper + lower) * 0.25
    zonal = middle[1]
    meridional = middle[2]
    mass_flux = 0.5 * ((MEAN_DEPTH + east_side[0]) * east_side[1] - (MEAN_DEPTH + west_side[0]) * west_side[1])
    mass_flux = mass_flux + 0.5 * ((MEAN_DEPTH + upper[0]) * upper[2] - (MEAN_DEPTH + lower[0]) * lower[2])
    height_dx = 0.5 * (east_side[0] - west_side[0])
    height_dy = 0.5 * (upper[0] - lower[0])
    zonal_dx = 0.5 * (east_side[1] - west_side[1])
    zonal_dy = 0.5 * (upper[1] - lower[1])
    merid_dx = 0.5 * (east_side[2] - west_side[2])
    merid_dy = 0.5 * (upper[2] - lower[2])
    new_height = average[0] - TIME_STEP * mass_flux
    new_zonal = average[1] - TIME_STEP * (zonal * zonal_dx + meridional * zonal_dy + GRAVITY * height_dx - CORIOLIS * meridional)
    new_merid = average[2] - TIME_STEP * (zonal * merid_dx + meridional * merid_dy + GRAVITY * height_dy + CORIOLIS * zonal)
    return jnp.stack([new_height, new_zonal, new_merid], axis=0)


def step_full(state_now):
    return tendency(state_now, jnp.roll(state_now, -1, axis=1), jnp.roll(state_now, 1, axis=1))


def advance(state_now):
    for _ in range(STEPS):
        state_now = step_full(state_now)
    return state_now


def apply_coarse(state_now, real_part, imag_part, height_part):
    height = state_now[..., 0, :, :] * height_part
    zonal = real_part * state_now[..., 1, :, :] + imag_part * state_now[..., 2, :, :]
    merid = real_part * state_now[..., 2, :, :] - imag_part * state_now[..., 1, :, :]
    return jnp.stack([height, zonal, merid], axis=-3)


def reference(states, initial_state, coarse_decay):
    prior = jnp.concatenate([initial_state[None], states[:-1]], axis=0)
    relaxed = lax.map(advance, prior)
    before = jnp.concatenate([initial_state[None], relaxed[:-1]], axis=0)
    ahead = lax.map(advance, before)
    residual = ahead - relaxed
    shrink = jnp.exp(-coarse_decay)
    real_part = shrink * jnp.cos(jnp.float32(TURN_ANGLE))
    imag_part = shrink * jnp.sin(jnp.float32(TURN_ANGLE))
    forcing = ahead - apply_coarse(before, real_part, imag_part, shrink)

    def chain(carried, term):
        following = apply_coarse(carried, real_part, imag_part, shrink) + term
        return following, following

    unused, corrected = lax.scan(chain, initial_state, forcing)
    return corrected, residual
```

```python
import functools

import jax
import jax.numpy as jnp
import numpy as np
from jax import lax
from jax.experimental import pallas as pl
from jax.experimental.pallas import tpu as pltpu
from jax.sharding import PartitionSpec as P

STEPS = 4
TIME_STEP = 0.25
CORIOLIS = 0.3
TURN_ANGLE = 1.2
LANES = 128
HALO = 2 * STEPS


def turns(blocks):
    turn = complex(np.cos(np.float32(TURN_ANGLE)), np.sin(np.float32(TURN_ANGLE)))
    powers = np.cumprod(np.full(blocks, turn, np.complex128))
    return np.repeat(np.concatenate([powers.real, powers.imag])[:, None], LANES, 1).astype(np.float32)


def fine_step(height, zonal, merid):
    rows = height.shape[0]
    lons = height.shape[1]

    def sides(a):
        return (
            pltpu.roll(a, lons - 1, 1),
            pltpu.roll(a, 1, 1),
            pltpu.roll(a, rows - 1, 0),
            pltpu.roll(a, 1, 0),
        )

    he, hw, hn, hs = sides(height)
    ze, zw, zn, zs = sides(zonal)
    me, mw, mn, ms = sides(merid)
    half = 0.5 * TIME_STEP
    flux = ((1.0 + he) * ze - (1.0 + hw) * zw) + ((1.0 + hn) * mn - (1.0 + hs) * ms)
    new_height = 0.25 * ((he + hw) + (hn + hs)) - half * flux
    new_zonal = (
        0.25 * ((ze + zw) + (zn + zs))
        - half * (zonal * (ze - zw) + merid * (zn - zs) + (he - hw))
        + (TIME_STEP * CORIOLIS) * merid
    )
    new_merid = (
        0.25 * ((me + mw) + (mn + ms))
        - half * (zonal * (me - mw) + merid * (mn - ms) + (hn - hs))
        - (TIME_STEP * CORIOLIS) * zonal
    )
    return new_height, new_zonal, new_merid


def turn_of(turn_ref, slot):
    blocks = turn_ref.shape[0] // 2
    return turn_ref[pl.ds(slot, 1)], turn_ref[pl.ds(slot + blocks, 1)]


def two_blocks(state):
    for _ in range(STEPS):
        state = fine_step(*state)
    relaxed = state
    for _ in range(STEPS):
        state = fine_step(*state)
    return relaxed, state


def forcing(turn_ref, decay, relaxed, ahead):
    blocks = turn_ref.shape[0] // 2
    mine = lax.axis_index("tm")
    shrink = jnp.where(mine == blocks - 1, 0.0, jnp.exp(-decay))
    cos1, sin1 = turn_of(turn_ref, 0)
    cos, sin = turn_of(turn_ref, lax.rem(mine + 2, blocks))
    height = ahead[0] - shrink * relaxed[0]
    zonal = ahead[1] - shrink * (cos1 * relaxed[1] + sin1 * relaxed[2])
    merid = ahead[2] - shrink * (cos1 * relaxed[2] - sin1 * relaxed[1])
    return height, cos * zonal - sin * merid, cos * merid + sin * zonal


def put_forcing(turn_ref, decay_ref, relaxed_ref, ahead_ref, term_ref, rows):
    lons = decay_ref.shape[1]
    per_plane = term_ref.shape[0] // 3
    for row in rows:
        for col in range(0, lons, LANES):
            where = (slice(row, row + 8), slice(col, col + LANES))
            relaxed = [relaxed_ref[(plane, *where)] for plane in range(3)]
            ahead = [ahead_ref[(plane, *where)] for plane in range(3)]
            at = row * lons // LANES + col * 8 // LANES
            for plane, term in enumerate(forcing(turn_ref, decay_ref[where], relaxed, ahead)):
                to = plane * per_plane + at
                term_ref[to : to + 8] = term


def inner_kernel(turn_ref, state_ref, decay_ref, term_ref, relaxed_ref, ahead_ref, term, sem):
    rows = state_ref.shape[1]
    relaxed, ahead = two_blocks([state_ref[plane] for plane in range(3)])
    for plane in range(3):
        relaxed_ref[plane] = relaxed[plane]
        ahead_ref[plane] = ahead[plane]
    put_forcing(turn_ref, decay_ref, relaxed_ref, ahead_ref, term, range(8, rows - 8, 8))
    edge = 8 * decay_ref.shape[1] // LANES
    per_plane = term.shape[0] // 3
    copies = []
    for plane in range(3):
        part = pl.ds(plane * per_plane + edge, per_plane - 2 * edge)
        copies.append(pltpu.make_async_copy(term.at[part], term_ref.at[part], sem.at[plane]))
        copies[-1].start()
    for copy in copies:
        copy.wait()


def edge_kernel(
    turn_ref, state_ref, first_ref, second_ref, decay_ref, term_in, relaxed_in, ahead_in,
    term_ref, relaxed_ref, ahead_ref, term, sem,
):
    even = lax.rem(lax.axis_index("lat"), 2) == 0
    rows = state_ref.shape[1]
    state = []
    for plane in range(3):
        first, second = first_ref[plane], second_ref[plane]
        below = jnp.where(even, second, first)
        above = jnp.where(even, first, second)
        low, high = state_ref[plane, : 2 * HALO], state_ref[plane, rows - 2 * HALO :]
        state.append(jnp.concatenate([below, low, high, above], axis=0))
    relaxed, ahead = two_blocks(state)
    for plane in range(3):
        for to, inner, value in (
            (relaxed_ref, relaxed_in, relaxed[plane]),
            (ahead_ref, ahead_in, ahead[plane]),
        ):
            to[plane, HALO : rows - HALO] = inner[plane, HALO : rows - HALO]
            to[plane, :HALO] = value[HALO : 2 * HALO]
            to[plane, rows - HALO :] = value[4 * HALO : 5 * HALO]
    put_forcing(turn_ref, decay_ref, relaxed_ref, ahead_ref, term, (0, rows - 8))
    edge = 8 * decay_ref.shape[1] // LANES
    per_plane = term.shape[0] // 3
    ends = [0, *(plane * per_plane for plane in (1, 2)), 3 * per_plane]
    copies = []
    for k, end in enumerate(ends):
        start, stop = max(end - edge, 0), min(end + edge, 3 * per_plane)
        part = pl.ds(start, stop - start)
        copies.append(pltpu.make_async_copy(term.at[part], term_ref.at[part], sem.at[k]))
        copies[-1].start()
    for copy in copies:
        copy.wait()


def solve_kernel(blocks, decay_ref, term_ref, value_ref, values, sem):
    shrink = jnp.exp(-decay_ref[...])
    each = shrink.shape[0]
    parts = sem.shape[0]

    def at(slot):
        return slice(slot * each, (slot + 1) * each)

    value = term_ref[at(blocks - 1)]
    copies = []
    for slot in range(blocks):
        if slot >= 2:
            value = shrink * value + term_ref[at(slot - 2)]
        values[at(slot)] = value
        if (slot + 1) % (blocks // parts) == 0:
            size = each * blocks // parts
            part = pl.ds(len(copies) * size, size)
            copies.append(pltpu.make_async_copy(values.at[part], value_ref.at[part], sem.at[len(copies)]))
            copies[-1].start()
    for copy in copies:
        copy.wait()


def residual_kernel(relaxed_ref, ahead_ref, residual_ref):
    first = lax.axis_index("tm") == 0
    for plane in range(3):
        relaxed = relaxed_ref[plane]
        residual_ref[0, plane] = jnp.where(first, relaxed, ahead_ref[plane]) - relaxed


def finish_kernel(turn_ref, value_ref, relaxed_ref, corrected_ref):
    mine = lax.axis_index("tm")
    first = mine == 0
    cos, sin = turn_of(turn_ref, mine)
    rows, lons = corrected_ref.shape[2:]
    per_plane = rows * lons // LANES
    at = 0
    for row in range(0, rows, 8):
        for col in range(0, lons, LANES):
            height, zonal, merid = (
                value_ref[plane * per_plane + at : plane * per_plane + at + 8] for plane in range(3)
            )
            values = (height, cos * zonal + sin * merid, cos * merid - sin * zonal)
            for plane in range(3):
                block = (plane, slice(row, row + 8), slice(col, col + LANES))
                corrected_ref[(0, *block)] = jnp.where(first, relaxed_ref[block], values[plane])
            at += 8


def on_device(states, initial_state, coarse_decay):
    blocks, slabs = lax.axis_size("tm"), lax.axis_size("lat")
    mine, slab = lax.axis_index("tm"), lax.axis_index("lat")
    _, planes, rows, lons = states.shape
    size = planes * rows * lons
    each = size // LANES // blocks
    vmem = pl.BlockSpec(memory_space=pltpu.VMEM)
    hbm = pl.BlockSpec(memory_space=pltpu.HBM)
    f32 = functools.partial(jax.ShapeDtypeStruct, dtype=jnp.float32)
    whole, flat = f32((planes, rows, lons)), f32((size // LANES, LANES))
    params = pltpu.CompilerParams(vmem_limit_bytes=32 << 20)
    turn = jnp.asarray(turns(blocks))

    def long(steps):
        return pl.CostEstimate(flops=steps * size, bytes_accessed=8 * size, transcendentals=0)

    state = jnp.where(mine == blocks - 1, initial_state, states[0])
    even = slab % 2 == 0
    low, high = state[:, :HALO], state[:, -HALO:]
    inner = [(i, i ^ 1) for i in range(slabs)]
    outer = [(i, (i - 1 if i % 2 == 0 else i + 1) % slabs) for i in range(slabs)]
    first = lax.ppermute(jnp.where(even, high, low), "lat", inner)
    second = lax.ppermute(jnp.where(even, low, high), "lat", outer)

    tiles = coarse_decay.reshape(rows // 8, 8, lons // LANES, LANES).transpose(0, 2, 1, 3)
    tiles = tiles.reshape(-1, LANES)
    tiles = jnp.concatenate([tiles, tiles[:each]], axis=0)
    own_decay = lax.dynamic_slice_in_dim(tiles, lax.rem(mine * each, rows * lons // LANES), each, 0)

    term, relaxed, ahead = pl.pallas_call(
        inner_kernel,
        out_shape=(flat, whole, whole),
        in_specs=[vmem] * 3,
        out_specs=(hbm, vmem, vmem),
        scratch_shapes=[pltpu.VMEM(flat.shape, jnp.float32), pltpu.SemaphoreType.DMA((3,))],
        compiler_params=params,
        cost_estimate=long(10**3),
    )(turn, state, coarse_decay)
    term, relaxed, ahead = pl.pallas_call(
        edge_kernel,
        out_shape=(flat, whole, whole),
        in_specs=[vmem] * 5 + [hbm, vmem, vmem],
        out_specs=(hbm, vmem, vmem),
        scratch_shapes=[pltpu.VMEM(flat.shape, jnp.float32), pltpu.SemaphoreType.DMA((4,))],
        input_output_aliases={5: 0},
        compiler_params=params,
    )(turn, state, first, second, coarse_decay, term, relaxed, ahead)

    def shifted(x, by):
        return lax.ppermute(x, "tm", [(i, (i + by) % blocks) for i in range(blocks)])

    relaxed, ahead = shifted(relaxed, 1), shifted(ahead, 2)
    residual = pl.pallas_call(
        residual_kernel,
        out_shape=f32((1, planes, rows, lons)),
        in_specs=[vmem, vmem],
        out_specs=vmem,
        compiler_params=params,
        cost_estimate=long(10**6),
    )(relaxed, ahead)
    term = lax.all_to_all(term.reshape(blocks, -1), "tm", 0, 0, tiled=True)
    value = pl.pallas_call(
        functools.partial(solve_kernel, blocks),
        out_shape=flat,
        in_specs=[vmem, vmem],
        out_specs=hbm,
        scratch_shapes=[pltpu.VMEM(flat.shape, jnp.float32), pltpu.SemaphoreType.DMA((4,))],
        compiler_params=params,
    )(own_decay, term.reshape(-1, LANES))
    value = lax.all_to_all(value.reshape(blocks, -1), "tm", 0, 0, tiled=True)
    corrected = pl.pallas_call(
        finish_kernel,
        out_shape=f32((1, planes, rows, lons)),
        in_specs=[vmem] * 3,
        out_specs=vmem,
        compiler_params=params,
    )(turn, value.reshape(-1, LANES), relaxed)
    return (corrected, residual)


def solution(mesh):
    placed = (P("tm", None, "lat", None), P(None, "lat", None), P("lat", None))
    return jax.shard_map(
        on_device,
        mesh=mesh,
        in_specs=placed,
        out_specs=(P("tm", None, "lat", None), P("tm", None, "lat", None)),
        check_vma=False,
    )
```

```python
import functools

import jax
import jax.numpy as jnp
import numpy as np
from jax import lax
from jax.experimental import pallas as pl
from jax.experimental.pallas import tpu as pltpu
from jax.sharding import PartitionSpec as P

STEPS = 4
TIME_STEP = 0.25
CORIOLIS = 0.3
TURN_ANGLE = 1.2
LANES = 128
HALO = 2 * STEPS


def turns(blocks):
    turn = complex(np.cos(np.float32(TURN_ANGLE)), np.sin(np.float32(TURN_ANGLE)))
    powers = np.cumprod(np.full(blocks, turn, np.complex128))
    return np.repeat(np.concatenate([powers.real, powers.imag])[:, None], LANES, 1).astype(np.float32)


def fine_step(height, zonal, merid):
    rows = height.shape[0]
    lons = height.shape[1]

    def sides(a):
        return (
            pltpu.roll(a, lons - 1, 1),
            pltpu.roll(a, 1, 1),
            pltpu.roll(a, rows - 1, 0),
            pltpu.roll(a, 1, 0),
        )

    he, hw, hn, hs = sides(height)
    ze, zw, zn, zs = sides(zonal)
    me, mw, mn, ms = sides(merid)
    half = 0.5 * TIME_STEP
    flux = ((1.0 + he) * ze - (1.0 + hw) * zw) + ((1.0 + hn) * mn - (1.0 + hs) * ms)
    new_height = 0.25 * ((he + hw) + (hn + hs)) - half * flux
    new_zonal = (
        0.25 * ((ze + zw) + (zn + zs))
        - half * (zonal * (ze - zw) + merid * (zn - zs) + (he - hw))
        + (TIME_STEP * CORIOLIS) * merid
    )
    new_merid = (
        0.25 * ((me + mw) + (mn + ms))
        - half * (zonal * (me - mw) + merid * (mn - ms) + (hn - hs))
        - (TIME_STEP * CORIOLIS) * zonal
    )
    return new_height, new_zonal, new_merid


def turn_of(turn_ref, slot):
    blocks = turn_ref.shape[0] // 2
    return turn_ref[pl.ds(slot, 1)], turn_ref[pl.ds(slot + blocks, 1)]


def two_blocks(state):
    for _ in range(STEPS):
        state = fine_step(*state)
    relaxed = state
    for _ in range(STEPS):
        state = fine_step(*state)
    return relaxed, state


def forcing(turn_ref, decay, relaxed, ahead):
    blocks = turn_ref.shape[0] // 2
    mine = lax.axis_index("tm")
    shrink = jnp.where(mine == blocks - 1, 0.0, jnp.exp(-decay))
    cos1, sin1 = turn_of(turn_ref, 0)
    cos, sin = turn_of(turn_ref, lax.rem(mine + 2, blocks))
    height = ahead[0] - shrink * relaxed[0]
    zonal = ahead[1] - shrink * (cos1 * relaxed[1] + sin1 * relaxed[2])
    merid = ahead[2] - shrink * (cos1 * relaxed[2] - sin1 * relaxed[1])
    return height, cos * zonal - sin * merid, cos * merid + sin * zonal


def put_forcing(turn_ref, decay_ref, relaxed_ref, ahead_ref, term_ref, rows):
    lons = decay_ref.shape[1]
    per_plane = term_ref.shape[0] // 3
    for row in rows:
        for col in range(0, lons, LANES):
            where = (slice(row, row + 8), slice(col, col + LANES))
            relaxed = [relaxed_ref[(plane, *where)] for plane in range(3)]
            ahead = [ahead_ref[(plane, *where)] for plane in range(3)]
            at = row * lons // LANES + col * 8 // LANES
            for plane, term in enumerate(forcing(turn_ref, decay_ref[where], relaxed, ahead)):
                to = plane * per_plane + at
                term_ref[to : to + 8] = term


def inner_kernel(turn_ref, state_ref, decay_ref, term_ref, relaxed_ref, ahead_ref, term, sem):
    rows = state_ref.shape[1]
    relaxed, ahead = two_blocks([state_ref[plane] for plane in range(3)])
    for plane in range(3):
        relaxed_ref[plane] = relaxed[plane]
        ahead_ref[plane] = ahead[plane]
    put_forcing(turn_ref, decay_ref, relaxed_ref, ahead_ref, term, range(8, rows - 8, 8))
    edge = 8 * decay_ref.shape[1] // LANES
    per_plane = term.shape[0] // 3
    copies = []
    for plane in range(3):
        part = pl.ds(plane * per_plane + edge, per_plane - 2 * edge)
        copies.append(pltpu.make_async_copy(term.at[part], term_ref.at[part], sem.at[plane]))
        copies[-1].start()
    for copy in copies:
        copy.wait()


def edge_kernel(
    turn_ref, state_ref, second_ref, first_ref, decay_ref, term_in, relaxed_in, ahead_in,
    term_ref, relaxed_ref, ahead_ref, term, sem,
):
    even = lax.rem(lax.axis_index("lat"), 2) == 0
    rows = state_ref.shape[1]
    state = []
    for plane in range(3):
        first, second = first_ref[plane], second_ref[plane]
        below = jnp.where(even, second, first)
        above = jnp.where(even, first, second)
        low, high = state_ref[plane, : 2 * HALO], state_ref[plane, rows - 2 * HALO :]
        state.append(jnp.concatenate([below, low, high, above], axis=0))
    relaxed, ahead = two_blocks(state)
    lons = decay_ref.shape[1]
    edge = 8 * lons // LANES
    per_plane = term.shape[0] // 3
    for row, at in ((0, HALO), (rows - 8, 4 * HALO)):
        for col in range(0, lons, LANES):
            cols = slice(col, col + LANES)
            tiles = [[a[at : at + 8, cols] for a in state] for state in (relaxed, ahead)]
            to = row * lons // LANES + col * 8 // LANES
            for plane, value in enumerate(forcing(turn_ref, decay_ref[row : row + 8, cols], *tiles)):
                term[plane * per_plane + to : plane * per_plane + to + 8] = value
    ends = [0, *(plane * per_plane for plane in (1, 2)), 3 * per_plane]
    copies = []
    for k, end in enumerate(ends):
        start, stop = max(end - edge, 0), min(end + edge, 3 * per_plane)
        part = pl.ds(start, stop - start)
        copies.append(pltpu.make_async_copy(term.at[part], term_ref.at[part], sem.at[k]))
        copies[-1].start()
    for to, inner, values in ((relaxed_ref, relaxed_in, relaxed), (ahead_ref, ahead_in, ahead)):
        for plane, value in enumerate(values):
            to[plane, HALO : rows - HALO] = inner[plane, HALO : rows - HALO]
            to[plane, :HALO] = value[HALO : 2 * HALO]
            to[plane, rows - HALO :] = value[4 * HALO : 5 * HALO]
    for copy in copies:
        copy.wait()


def solve_kernel(blocks, lead, decay_ref, term_ref, value_ref, values, sem):
    shrink = jnp.exp(-decay_ref[...])
    each = shrink.shape[0]
    parts = sem.shape[0]

    def at(slot):
        place = (slot - lead) % blocks
        return slice(place * each, (place + 1) * each)

    value = term_ref[at(blocks - 1)]
    size = each * blocks // parts
    copies, done = [], set()
    for slot in range(blocks):
        if slot >= 2:
            value = shrink * value + term_ref[at(slot - 2)]
        values[at(slot)] = value
        done.add((slot - lead) % blocks * parts // blocks)
        later = {(more - lead) % blocks * parts // blocks for more in range(slot + 1, blocks)}
        for k in sorted(done - later):
            done.remove(k)
            part = pl.ds(k * size, size)
            copies.append(pltpu.make_async_copy(values.at[part], value_ref.at[part], sem.at[k]))
            copies[-1].start()
    for copy in copies:
        copy.wait()


def residual_kernel(relaxed_ref, ahead_ref, residual_ref):
    first = lax.axis_index("tm") == 0
    for plane in range(3):
        relaxed = relaxed_ref[plane]
        residual_ref[0, plane] = jnp.where(first, relaxed, ahead_ref[plane]) - relaxed


def finish_kernel(turn_ref, value_ref, relaxed_ref, corrected_ref):
    mine = lax.axis_index("tm")
    first = mine == 0
    cos, sin = turn_of(turn_ref, mine)
    rows, lons = corrected_ref.shape[2:]
    per_plane = rows * lons // LANES
    at = 0
    for row in range(0, rows, 8):
        for col in range(0, lons, LANES):
            height, zonal, merid = (
                value_ref[plane * per_plane + at : plane * per_plane + at + 8] for plane in range(3)
            )
            values = (height, cos * zonal + sin * merid, cos * merid - sin * zonal)
            for plane in range(3):
                block = (plane, slice(row, row + 8), slice(col, col + LANES))
                corrected_ref[(0, *block)] = jnp.where(first, relaxed_ref[block], values[plane])
            at += 8


def on_device(states, initial_state, coarse_decay):
    blocks, slabs = lax.axis_size("tm"), lax.axis_size("lat")
    mine, slab = lax.axis_index("tm"), lax.axis_index("lat")
    _, planes, rows, lons = states.shape
    size = planes * rows * lons
    each = size // LANES // blocks
    vmem = pl.BlockSpec(memory_space=pltpu.VMEM)
    hbm = pl.BlockSpec(memory_space=pltpu.HBM)
    f32 = functools.partial(jax.ShapeDtypeStruct, dtype=jnp.float32)
    whole, flat = f32((planes, rows, lons)), f32((size // LANES, LANES))
    params = pltpu.CompilerParams(vmem_limit_bytes=32 << 20)
    turn = jnp.asarray(turns(blocks))
    lead = 5 * blocks // 8
    places = [[(place + lead) % blocks for place in range(blocks)]]

    def exchanged(x):
        return lax.all_to_all(
            x.reshape(blocks, -1), "tm", 0, 0, axis_index_groups=places, tiled=True
        ).reshape(-1, LANES)

    def long(steps):
        return pl.CostEstimate(flops=steps * size, bytes_accessed=8 * size, transcendentals=0)

    state = jnp.where(mine == blocks - 1, initial_state, states[0])
    even = slab % 2 == 0
    low, high = state[:, :HALO], state[:, -HALO:]
    inner = [(i, i ^ 1) for i in range(slabs)]
    outer = [(i, (i - 1 if i % 2 == 0 else i + 1) % slabs) for i in range(slabs)]
    second = lax.ppermute(jnp.where(even, low, high), "lat", outer)
    first = lax.ppermute(jnp.where(even, high, low), "lat", inner)

    tiles = coarse_decay.reshape(rows // 8, 8, lons // LANES, LANES).transpose(0, 2, 1, 3)
    tiles = tiles.reshape(-1, LANES)
    tiles = jnp.concatenate([tiles, tiles[:each]], axis=0)
    place = lax.rem(mine + blocks - lead, blocks)
    own_decay = lax.dynamic_slice_in_dim(tiles, lax.rem(place * each, rows * lons // LANES), each, 0)

    term, relaxed, ahead = pl.pallas_call(
        inner_kernel,
        out_shape=(flat, whole, whole),
        in_specs=[vmem] * 3,
        out_specs=(hbm, vmem, vmem),
        scratch_shapes=[pltpu.VMEM(flat.shape, jnp.float32), pltpu.SemaphoreType.DMA((3,))],
        compiler_params=params,
        cost_estimate=long(10**3),
    )(turn, state, coarse_decay)
    term, relaxed, ahead = pl.pallas_call(
        edge_kernel,
        out_shape=(flat, whole, whole),
        in_specs=[vmem] * 5 + [hbm, vmem, vmem],
        out_specs=(hbm, vmem, vmem),
        scratch_shapes=[pltpu.VMEM(flat.shape, jnp.float32), pltpu.SemaphoreType.DMA((4,))],
        input_output_aliases={5: 0},
        compiler_params=params,
    )(turn, state, second, first, coarse_decay, term, relaxed, ahead)

    def shifted(x, by):
        return lax.ppermute(x, "tm", [(i, (i + by) % blocks) for i in range(blocks)])

    relaxed, ahead = shifted(relaxed, 1), shifted(ahead, 2)
    residual = pl.pallas_call(
        residual_kernel,
        out_shape=f32((1, planes, rows, lons)),
        in_specs=[vmem, vmem],
        out_specs=vmem,
        compiler_params=params,
        cost_estimate=long(10**6),
    )(relaxed, ahead)
    value = pl.pallas_call(
        functools.partial(solve_kernel, blocks, lead),
        out_shape=flat,
        in_specs=[vmem, vmem],
        out_specs=hbm,
        scratch_shapes=[pltpu.VMEM(flat.shape, jnp.float32), pltpu.SemaphoreType.DMA((4,))],
        compiler_params=params,
    )(own_decay, exchanged(term))
    corrected = pl.pallas_call(
        finish_kernel,
        out_shape=f32((1, planes, rows, lons)),
        in_specs=[vmem] * 3,
        out_specs=vmem,
        compiler_params=params,
    )(turn, exchanged(value), relaxed)
    return (corrected, residual)


def solution(mesh):
    placed = (P("tm", None, "lat", None), P(None, "lat", None), P("lat", None))
    return jax.shard_map(
        on_device,
        mesh=mesh,
        in_specs=placed,
        out_specs=(P("tm", None, "lat", None), P("tm", None, "lat", None)),
        check_vma=False,
    )
```

```python
import functools

import jax
import jax.numpy as jnp
import numpy as np
from jax import lax
from jax.experimental import pallas as pl
from jax.experimental.pallas import tpu as pltpu
from jax.sharding import PartitionSpec as P

STEPS = 4
TIME_STEP = 0.25
CORIOLIS = 0.3
TURN_ANGLE = 1.2
LANES = 128
HALO = 2 * STEPS


def turns(blocks):
    turn = complex(np.cos(np.float32(TURN_ANGLE)), np.sin(np.float32(TURN_ANGLE)))
    powers = np.cumprod(np.full(blocks, turn, np.complex128))
    return np.repeat(np.concatenate([powers.real, powers.imag])[:, None], LANES, 1).astype(np.float32)


def fine_step(height, zonal, merid):
    rows = height.shape[0]
    lons = height.shape[1]

    def sides(a):
        return (
            pltpu.roll(a, lons - 1, 1),
            pltpu.roll(a, 1, 1),
            pltpu.roll(a, rows - 1, 0),
            pltpu.roll(a, 1, 0),
        )

    he, hw, hn, hs = sides(height)
    ze, zw, zn, zs = sides(zonal)
    me, mw, mn, ms = sides(merid)
    half = 0.5 * TIME_STEP
    flux = ((1.0 + he) * ze - (1.0 + hw) * zw) + ((1.0 + hn) * mn - (1.0 + hs) * ms)
    new_height = 0.25 * ((he + hw) + (hn + hs)) - half * flux
    new_zonal = (
        0.25 * ((ze + zw) + (zn + zs))
        - half * (zonal * (ze - zw) + merid * (zn - zs) + (he - hw))
        + (TIME_STEP * CORIOLIS) * merid
    )
    new_merid = (
        0.25 * ((me + mw) + (mn + ms))
        - half * (zonal * (me - mw) + merid * (mn - ms) + (hn - hs))
        - (TIME_STEP * CORIOLIS) * zonal
    )
    return new_height, new_zonal, new_merid


def turn_of(turn_ref, slot):
    blocks = turn_ref.shape[0] // 2
    return turn_ref[pl.ds(slot, 1)], turn_ref[pl.ds(slot + blocks, 1)]


def two_blocks(state):
    for _ in range(STEPS):
        state = fine_step(*state)
    relaxed = state
    for _ in range(STEPS):
        state = fine_step(*state)
    return relaxed, state


def forcing(turn_ref, decay, relaxed, ahead):
    blocks = turn_ref.shape[0] // 2
    mine = lax.axis_index("tm")
    shrink = jnp.where(mine == blocks - 1, 0.0, jnp.exp(-decay))
    cos1, sin1 = turn_of(turn_ref, 0)
    cos, sin = turn_of(turn_ref, lax.rem(mine + 2, blocks))
    height = ahead[0] - shrink * relaxed[0]
    zonal = ahead[1] - shrink * (cos1 * relaxed[1] + sin1 * relaxed[2])
    merid = ahead[2] - shrink * (cos1 * relaxed[2] - sin1 * relaxed[1])
    return height, cos * zonal - sin * merid, cos * merid + sin * zonal


def put_forcing(turn_ref, decay_ref, relaxed_ref, ahead_ref, term_ref, rows):
    lons = decay_ref.shape[1]
    per_plane = term_ref.shape[0] // 3
    for row in rows:
        for col in range(0, lons, LANES):
            where = (slice(row, row + 8), slice(col, col + LANES))
            relaxed = [relaxed_ref[(plane, *where)] for plane in range(3)]
            ahead = [ahead_ref[(plane, *where)] for plane in range(3)]
            at = row * lons // LANES + col * 8 // LANES
            for plane, term in enumerate(forcing(turn_ref, decay_ref[where], relaxed, ahead)):
                to = plane * per_plane + at
                term_ref[to : to + 8] = term


def inner_kernel(turn_ref, state_ref, decay_ref, term_ref, relaxed_ref, ahead_ref, term, sem):
    rows = state_ref.shape[1]
    relaxed, ahead = two_blocks([state_ref[plane] for plane in range(3)])
    for plane in range(3):
        relaxed_ref[plane] = relaxed[plane]
        ahead_ref[plane] = ahead[plane]
    put_forcing(turn_ref, decay_ref, relaxed_ref, ahead_ref, term, range(8, rows - 8, 8))
    edge = 8 * decay_ref.shape[1] // LANES
    per_plane = term.shape[0] // 3
    copies = []
    for plane in range(3):
        part = pl.ds(plane * per_plane + edge, per_plane - 2 * edge)
        copies.append(pltpu.make_async_copy(term.at[part], term_ref.at[part], sem.at[plane]))
        copies[-1].start()
    for copy in copies:
        copy.wait()


def edge_kernel(
    turn_ref, state_ref, second_ref, first_ref, decay_ref, term_in, relaxed_in, ahead_in,
    term_ref, relaxed_ref, ahead_ref, term, sem,
):
    even = lax.rem(lax.axis_index("lat"), 2) == 0
    rows = state_ref.shape[1]
    state = []
    for plane in range(3):
        first, second = first_ref[plane], second_ref[plane]
        below = jnp.where(even, second, first)
        above = jnp.where(even, first, second)
        low, high = state_ref[plane, : 2 * HALO], state_ref[plane, rows - 2 * HALO :]
        state.append(jnp.concatenate([below, low, high, above], axis=0))
    relaxed, ahead = two_blocks(state)
    lons = decay_ref.shape[1]
    edge = 8 * lons // LANES
    per_plane = term.shape[0] // 3
    for row, at in ((0, HALO), (rows - 8, 4 * HALO)):
        for col in range(0, lons, LANES):
            cols = slice(col, col + LANES)
            tiles = [[a[at : at + 8, cols] for a in state] for state in (relaxed, ahead)]
            to = row * lons // LANES + col * 8 // LANES
            for plane, value in enumerate(forcing(turn_ref, decay_ref[row : row + 8, cols], *tiles)):
                term[plane * per_plane + to : plane * per_plane + to + 8] = value
    ends = [0, *(plane * per_plane for plane in (1, 2)), 3 * per_plane]
    copies = []
    for k, end in enumerate(ends):
        start, stop = max(end - edge, 0), min(end + edge, 3 * per_plane)
        part = pl.ds(start, stop - start)
        copies.append(pltpu.make_async_copy(term.at[part], term_ref.at[part], sem.at[k]))
        copies[-1].start()
    for to, inner, values in ((relaxed_ref, relaxed_in, relaxed), (ahead_ref, ahead_in, ahead)):
        for plane, value in enumerate(values):
            to[plane, HALO : rows - HALO] = inner[plane, HALO : rows - HALO]
            to[plane, :HALO] = value[HALO : 2 * HALO]
            to[plane, rows - HALO :] = value[4 * HALO : 5 * HALO]
    for copy in copies:
        copy.wait()


def solve_kernel(places, decay_ref, term_ref, value_ref, values, sem):
    shrink = jnp.exp(-decay_ref[...])
    each = shrink.shape[0]
    parts = sem.shape[0]

    blocks = len(places)

    def at(slot):
        return slice(places[slot] * each, (places[slot] + 1) * each)

    value = term_ref[at(blocks - 1)]
    size = each * blocks // parts
    copies, done = [], set()
    for slot in range(blocks):
        if slot >= 2:
            value = shrink * value + term_ref[at(slot - 2)]
        values[at(slot)] = value
        done.add(places[slot] * parts // blocks)
        later = {place * parts // blocks for place in places[slot + 1 :]}
        for k in sorted(done - later):
            done.remove(k)
            part = pl.ds(k * size, size)
            copies.append(pltpu.make_async_copy(values.at[part], value_ref.at[part], sem.at[k]))
            copies[-1].start()
    for copy in copies:
        copy.wait()


def residual_kernel(relaxed_ref, ahead_ref, residual_ref):
    first = lax.axis_index("tm") == 0
    for plane in range(3):
        relaxed = relaxed_ref[plane]
        residual_ref[0, plane] = jnp.where(first, relaxed, ahead_ref[plane]) - relaxed


def finish_kernel(turn_ref, value_ref, relaxed_ref, corrected_ref):
    mine = lax.axis_index("tm")
    first = mine == 0
    cos, sin = turn_of(turn_ref, mine)
    rows, lons = corrected_ref.shape[2:]
    per_plane = rows * lons // LANES
    at = 0
    for row in range(0, rows, 8):
        for col in range(0, lons, LANES):
            height, zonal, merid = (
                value_ref[plane * per_plane + at : plane * per_plane + at + 8] for plane in range(3)
            )
            values = (height, cos * zonal + sin * merid, cos * merid - sin * zonal)
            for plane in range(3):
                block = (plane, slice(row, row + 8), slice(col, col + LANES))
                corrected_ref[(0, *block)] = jnp.where(first, relaxed_ref[block], values[plane])
            at += 8


def on_device(states, initial_state, coarse_decay):
    blocks, slabs = lax.axis_size("tm"), lax.axis_size("lat")
    mine, slab = lax.axis_index("tm"), lax.axis_index("lat")
    _, planes, rows, lons = states.shape
    size = planes * rows * lons
    each = size // LANES // blocks
    vmem = pl.BlockSpec(memory_space=pltpu.VMEM)
    hbm = pl.BlockSpec(memory_space=pltpu.HBM)
    f32 = functools.partial(jax.ShapeDtypeStruct, dtype=jnp.float32)
    whole, flat = f32((planes, rows, lons)), f32((size // LANES, LANES))
    params = pltpu.CompilerParams(vmem_limit_bytes=32 << 20)
    turn = jnp.asarray(turns(blocks))
    lead = 11 * blocks // 16
    order = [lead] + [block for block in range(blocks) if block != lead]
    places = [order.index(block) for block in range(blocks)]

    def exchanged(x):
        return lax.all_to_all(
            x.reshape(blocks, -1), "tm", 0, 0, axis_index_groups=[order], tiled=True
        ).reshape(-1, LANES)

    def long(steps):
        return pl.CostEstimate(flops=steps * size, bytes_accessed=8 * size, transcendentals=0)

    state = jnp.where(mine == blocks - 1, initial_state, states[0])
    even = slab % 2 == 0
    low, high = state[:, :HALO], state[:, -HALO:]
    inner = [(i, i ^ 1) for i in range(slabs)]
    outer = [(i, (i - 1 if i % 2 == 0 else i + 1) % slabs) for i in range(slabs)]
    second = lax.ppermute(jnp.where(even, low, high), "lat", outer)
    first = lax.ppermute(jnp.where(even, high, low), "lat", inner)

    tiles = coarse_decay.reshape(rows // 8, 8, lons // LANES, LANES).transpose(0, 2, 1, 3)
    tiles = tiles.reshape(-1, LANES)
    tiles = jnp.concatenate([tiles, tiles[:each]], axis=0)
    place = jnp.where(mine == lead, 0, jnp.where(mine < lead, mine + 1, mine))
    own_decay = lax.dynamic_slice_in_dim(tiles, lax.rem(place * each, rows * lons // LANES), each, 0)

    term, relaxed, ahead = pl.pallas_call(
        inner_kernel,
        out_shape=(flat, whole, whole),
        in_specs=[vmem] * 3,
        out_specs=(hbm, vmem, vmem),
        scratch_shapes=[pltpu.VMEM(flat.shape, jnp.float32), pltpu.SemaphoreType.DMA((3,))],
        compiler_params=params,
        cost_estimate=long(10**3),
    )(turn, state, coarse_decay)
    term, relaxed, ahead = pl.pallas_call(
        edge_kernel,
        out_shape=(flat, whole, whole),
        in_specs=[vmem] * 5 + [hbm, vmem, vmem],
        out_specs=(hbm, vmem, vmem),
        scratch_shapes=[pltpu.VMEM(flat.shape, jnp.float32), pltpu.SemaphoreType.DMA((4,))],
        input_output_aliases={5: 0},
        compiler_params=params,
    )(turn, state, second, first, coarse_decay, term, relaxed, ahead)

    relaxed = lax.ppermute(relaxed, "tm", [(i, (i + 1) % blocks) for i in range(blocks)])
    ahead = lax.ppermute(ahead, "tm", [(i, (i + 2) % blocks) for i in range(blocks) if i != blocks - 2])
    residual = pl.pallas_call(
        residual_kernel,
        out_shape=f32((1, planes, rows, lons)),
        in_specs=[vmem, vmem],
        out_specs=vmem,
        compiler_params=params,
        cost_estimate=long(10**6),
    )(relaxed, ahead)
    value = pl.pallas_call(
        functools.partial(solve_kernel, places),
        out_shape=flat,
        in_specs=[vmem, vmem],
        out_specs=hbm,
        scratch_shapes=[pltpu.VMEM(flat.shape, jnp.float32), pltpu.SemaphoreType.DMA((4,))],
        compiler_params=params,
    )(own_decay, exchanged(term))
    corrected = pl.pallas_call(
        finish_kernel,
        out_shape=f32((1, planes, rows, lons)),
        in_specs=[vmem] * 3,
        out_specs=vmem,
        compiler_params=params,
    )(turn, exchanged(value), relaxed)
    return (corrected, residual)


def solution(mesh):
    placed = (P("tm", None, "lat", None), P(None, "lat", None), P("lat", None))
    return jax.shard_map(
        on_device,
        mesh=mesh,
        in_specs=placed,
        out_specs=(P("tm", None, "lat", None), P("tm", None, "lat", None)),
        check_vma=False,
    )
```

```python
import functools

import jax
import jax.numpy as jnp
import numpy as np
from jax import lax
from jax.experimental import pallas as pl
from jax.experimental.pallas import tpu as pltpu
from jax.sharding import PartitionSpec as P

STEPS = 4
TIME_STEP = 0.25
CORIOLIS = 0.3
TURN_ANGLE = 1.2
LANES = 128
HALO = 2 * STEPS


def turns(blocks):
    turn = complex(np.cos(np.float32(TURN_ANGLE)), np.sin(np.float32(TURN_ANGLE)))
    powers = np.cumprod(np.full(blocks, turn, np.complex128))
    return np.repeat(np.concatenate([powers.real, powers.imag])[:, None], LANES, 1).astype(np.float32)


def fine_step(height, zonal, merid):
    rows = height.shape[0]
    lons = height.shape[1]

    def sides(a):
        return (
            pltpu.roll(a, lons - 1, 1),
            pltpu.roll(a, 1, 1),
            pltpu.roll(a, rows - 1, 0),
            pltpu.roll(a, 1, 0),
        )

    he, hw, hn, hs = sides(height)
    ze, zw, zn, zs = sides(zonal)
    me, mw, mn, ms = sides(merid)
    half = 0.5 * TIME_STEP
    flux = ((1.0 + he) * ze - (1.0 + hw) * zw) + ((1.0 + hn) * mn - (1.0 + hs) * ms)
    new_height = 0.25 * ((he + hw) + (hn + hs)) - half * flux
    new_zonal = (
        0.25 * ((ze + zw) + (zn + zs))
        - half * (zonal * (ze - zw) + merid * (zn - zs) + (he - hw))
        + (TIME_STEP * CORIOLIS) * merid
    )
    new_merid = (
        0.25 * ((me + mw) + (mn + ms))
        - half * (zonal * (me - mw) + merid * (mn - ms) + (hn - hs))
        - (TIME_STEP * CORIOLIS) * zonal
    )
    return new_height, new_zonal, new_merid


def turn_of(turn_ref, slot):
    blocks = turn_ref.shape[0] // 2
    return turn_ref[pl.ds(slot, 1)], turn_ref[pl.ds(slot + blocks, 1)]


def two_blocks(state):
    for _ in range(STEPS):
        state = fine_step(*state)
    relaxed = state
    for _ in range(STEPS):
        state = fine_step(*state)
    return relaxed, state


def forcing(turn_ref, decay, relaxed, ahead):
    blocks = turn_ref.shape[0] // 2
    mine = lax.axis_index("tm")
    shrink = jnp.where(mine == blocks - 1, 0.0, jnp.exp(-decay))
    cos1, sin1 = turn_of(turn_ref, 0)
    cos, sin = turn_of(turn_ref, lax.rem(mine + 2, blocks))
    height = ahead[0] - shrink * relaxed[0]
    zonal = ahead[1] - shrink * (cos1 * relaxed[1] + sin1 * relaxed[2])
    merid = ahead[2] - shrink * (cos1 * relaxed[2] - sin1 * relaxed[1])
    return height, cos * zonal - sin * merid, cos * merid + sin * zonal


def put_forcing(turn_ref, decay_ref, relaxed_ref, ahead_ref, term_ref, rows):
    lons = decay_ref.shape[1]
    per_plane = term_ref.shape[0] // 3
    for row in rows:
        for col in range(0, lons, LANES):
            where = (slice(row, row + 8), slice(col, col + LANES))
            relaxed = [relaxed_ref[(plane, *where)] for plane in range(3)]
            ahead = [ahead_ref[(plane, *where)] for plane in range(3)]
            at = row * lons // LANES + col * 8 // LANES
            for plane, term in enumerate(forcing(turn_ref, decay_ref[where], relaxed, ahead)):
                to = plane * per_plane + at
                term_ref[to : to + 8] = term


def relax_kernel(
    turn_ref, state_ref, second_ref, pair_ref, decay_ref, term_ref, relaxed_ref, ahead_ref, term, sem
):
    even = lax.rem(lax.axis_index("lat"), 2) == 0
    rows, lons = state_ref.shape[1:]
    state = []
    for plane in range(3):
        first = jnp.where(even, pair_ref[1, plane], pair_ref[0, plane])
        second = second_ref[plane]
        below = jnp.where(even, second, first)
        above = jnp.where(even, first, second)
        state.append(jnp.concatenate([below, state_ref[plane], above], axis=0))
    relaxed, ahead = two_blocks(state)
    per_plane = term.shape[0] // 3
    for row in range(0, rows, 8):
        for col in range(0, lons, LANES):
            cols = slice(col, col + LANES)
            at = row + HALO
            tiles = [[a[at : at + 8, cols] for a in state] for state in (relaxed, ahead)]
            to = row * lons // LANES + col * 8 // LANES
            for plane, value in enumerate(forcing(turn_ref, decay_ref[row : row + 8, cols], *tiles)):
                term[plane * per_plane + to : plane * per_plane + to + 8] = value
    copy = pltpu.make_async_copy(term, term_ref, sem.at[0])
    copy.start()
    for to, values in ((relaxed_ref, relaxed), (ahead_ref, ahead)):
        for plane, value in enumerate(values):
            to[plane] = value[HALO : HALO + rows]
    copy.wait()


def solve_kernel(places, decay_ref, term_ref, value_ref, values, sem):
    shrink = jnp.exp(-decay_ref[...])
    each = shrink.shape[0]
    parts = sem.shape[0]

    blocks = len(places)

    def at(slot):
        return slice(places[slot] * each, (places[slot] + 1) * each)

    value = term_ref[at(blocks - 1)]
    size = each * blocks // parts
    copies, done = [], set()
    for slot in range(blocks):
        if slot >= 2:
            value = shrink * value + term_ref[at(slot - 2)]
        values[at(slot)] = value
        done.add(places[slot] * parts // blocks)
        later = {place * parts // blocks for place in places[slot + 1 :]}
        for k in sorted(done - later):
            done.remove(k)
            part = pl.ds(k * size, size)
            copies.append(pltpu.make_async_copy(values.at[part], value_ref.at[part], sem.at[k]))
            copies[-1].start()
    for copy in copies:
        copy.wait()


def pass_kernel(blocks, both_ref, ahead_ref, passed_ref):
    mine = lax.axis_index("tm")
    odd = lax.rem(mine, 2) == 1
    last = mine == blocks - 2
    for plane in range(3):
        ahead, other = ahead_ref[plane], both_ref[1, plane]
        passed_ref[plane] = jnp.where(odd, ahead, jnp.where(last, other, ahead - other))


def residual_kernel(both_ref, got_ref, residual_ref):
    mine = lax.axis_index("tm")
    odd, first = lax.rem(mine, 2) == 1, mine == 0
    for plane in range(3):
        got = got_ref[plane]
        relaxed = jnp.where(odd, both_ref[0, plane], jnp.where(first, got, 0.0))
        residual_ref[0, plane] = got - relaxed


def finish_kernel(turn_ref, value_ref, got_ref, corrected_ref):
    mine = lax.axis_index("tm")
    first = mine == 0
    cos, sin = turn_of(turn_ref, mine)
    rows, lons = corrected_ref.shape[2:]
    per_plane = rows * lons // LANES
    at = 0
    for row in range(0, rows, 8):
        for col in range(0, lons, LANES):
            height, zonal, merid = (
                value_ref[plane * per_plane + at : plane * per_plane + at + 8] for plane in range(3)
            )
            values = (height, cos * zonal + sin * merid, cos * merid - sin * zonal)
            for plane in range(3):
                block = (plane, slice(row, row + 8), slice(col, col + LANES))
                corrected_ref[(0, *block)] = jnp.where(first, got_ref[block], values[plane])
            at += 8


def on_device(states, initial_state, coarse_decay):
    blocks, slabs = lax.axis_size("tm"), lax.axis_size("lat")
    mine, slab = lax.axis_index("tm"), lax.axis_index("lat")
    _, planes, rows, lons = states.shape
    size = planes * rows * lons
    each = size // LANES // blocks
    vmem = pl.BlockSpec(memory_space=pltpu.VMEM)
    hbm = pl.BlockSpec(memory_space=pltpu.HBM)
    f32 = functools.partial(jax.ShapeDtypeStruct, dtype=jnp.float32)
    whole, flat = f32((planes, rows, lons)), f32((size // LANES, LANES))
    params = pltpu.CompilerParams(vmem_limit_bytes=32 << 20)
    turn = jnp.asarray(turns(blocks))
    lead = 11 * blocks // 16
    order = [lead] + [block for block in range(blocks) if block != lead]
    places = [order.index(block) for block in range(blocks)]

    def exchanged(x):
        return lax.all_to_all(
            x.reshape(blocks, -1), "tm", 0, 0, axis_index_groups=[order], tiled=True
        ).reshape(-1, LANES)

    def long(steps):
        return pl.CostEstimate(flops=steps * size, bytes_accessed=8 * size, transcendentals=0)

    state = jnp.where(mine == blocks - 1, initial_state, states[0])
    even = slab % 2 == 0
    low, high = state[:, :HALO], state[:, -HALO:]
    outer = [(i, (i - 1 if i % 2 == 0 else i + 1) % slabs) for i in range(slabs)]
    second = lax.ppermute(jnp.where(even, low, high), "lat", outer)
    pairs = [[i, i + 1] for i in range(0, slabs, 2)]
    pair = lax.all_gather(jnp.where(even, high, low), "lat", axis_index_groups=pairs)

    tiles = coarse_decay.reshape(rows // 8, 8, lons // LANES, LANES).transpose(0, 2, 1, 3)
    tiles = tiles.reshape(-1, LANES)
    tiles = jnp.concatenate([tiles, tiles[:each]], axis=0)
    place = jnp.where(mine == lead, 0, jnp.where(mine < lead, mine + 1, mine))
    own_decay = lax.dynamic_slice_in_dim(tiles, lax.rem(place * each, rows * lons // LANES), each, 0)

    term, relaxed, ahead = pl.pallas_call(
        relax_kernel,
        out_shape=(flat, whole, whole),
        in_specs=[vmem] * 5,
        out_specs=(hbm, vmem, vmem),
        scratch_shapes=[pltpu.VMEM(flat.shape, jnp.float32), pltpu.SemaphoreType.DMA((1,))],
        compiler_params=params,
    )(turn, state, second, pair, coarse_decay)

    both = lax.all_gather(relaxed, "tm", axis_index_groups=[[i, i + 1] for i in range(0, blocks, 2)])
    passed = pl.pallas_call(
        functools.partial(pass_kernel, blocks),
        out_shape=whole,
        in_specs=[vmem, vmem],
        out_specs=vmem,
        compiler_params=params,
    )(both, ahead)
    got = lax.ppermute(passed, "tm", [(i, (i + 2) % blocks) for i in range(blocks)])
    residual = pl.pallas_call(
        residual_kernel,
        out_shape=f32((1, planes, rows, lons)),
        in_specs=[vmem, vmem],
        out_specs=vmem,
        compiler_params=params,
        cost_estimate=long(10**6),
    )(both, got)
    value = pl.pallas_call(
        functools.partial(solve_kernel, places),
        out_shape=flat,
        in_specs=[vmem, vmem],
        out_specs=hbm,
        scratch_shapes=[pltpu.VMEM(flat.shape, jnp.float32), pltpu.SemaphoreType.DMA((4,))],
        compiler_params=params,
    )(own_decay, exchanged(term))
    corrected = pl.pallas_call(
        finish_kernel,
        out_shape=f32((1, planes, rows, lons)),
        in_specs=[vmem] * 3,
        out_specs=vmem,
        compiler_params=params,
    )(turn, exchanged(value), got)
    return (corrected, residual)


def solution(mesh):
    placed = (P("tm", None, "lat", None), P(None, "lat", None), P("lat", None))
    return jax.shard_map(
        on_device,
        mesh=mesh,
        in_specs=placed,
        out_specs=(P("tm", None, "lat", None), P("tm", None, "lat", None)),
        check_vma=False,
    )
```

```python
import functools

import jax
import jax.numpy as jnp
import numpy as np
from jax import lax
from jax.experimental import pallas as pl
from jax.experimental.pallas import tpu as pltpu
from jax.sharding import PartitionSpec as P

STEPS = 4
TIME_STEP = 0.25
CORIOLIS = 0.3
TURN_ANGLE = 1.2
LANES = 128
HALO = 2 * STEPS


def turns(blocks):
    turn = complex(np.cos(np.float32(TURN_ANGLE)), np.sin(np.float32(TURN_ANGLE)))
    powers = np.cumprod(np.full(blocks, turn, np.complex128))
    return np.repeat(np.concatenate([powers.real, powers.imag])[:, None], LANES, 1).astype(np.float32)


def fine_step(height, zonal, merid):
    rows = height.shape[0]
    lons = height.shape[1]

    def sides(a):
        return (
            pltpu.roll(a, lons - 1, 1),
            pltpu.roll(a, 1, 1),
            pltpu.roll(a, rows - 1, 0),
            pltpu.roll(a, 1, 0),
        )

    he, hw, hn, hs = sides(height)
    ze, zw, zn, zs = sides(zonal)
    me, mw, mn, ms = sides(merid)
    half = 0.5 * TIME_STEP
    flux = ((1.0 + he) * ze - (1.0 + hw) * zw) + ((1.0 + hn) * mn - (1.0 + hs) * ms)
    new_height = 0.25 * ((he + hw) + (hn + hs)) - half * flux
    new_zonal = (
        0.25 * ((ze + zw) + (zn + zs))
        - half * (zonal * (ze - zw) + merid * (zn - zs) + (he - hw))
        + (TIME_STEP * CORIOLIS) * merid
    )
    new_merid = (
        0.25 * ((me + mw) + (mn + ms))
        - half * (zonal * (me - mw) + merid * (mn - ms) + (hn - hs))
        - (TIME_STEP * CORIOLIS) * zonal
    )
    return new_height, new_zonal, new_merid


def turn_of(turn_ref, slot):
    blocks = turn_ref.shape[0] // 2
    return turn_ref[pl.ds(slot, 1)], turn_ref[pl.ds(slot + blocks, 1)]


def two_blocks(state):
    for _ in range(STEPS):
        state = fine_step(*state)
    relaxed = state
    for _ in range(STEPS):
        state = fine_step(*state)
    return relaxed, state


def forcing(turn_ref, decay, relaxed, ahead):
    blocks = turn_ref.shape[0] // 2
    mine = lax.axis_index("tm")
    shrink = jnp.where(mine == blocks - 1, 0.0, jnp.exp(-decay))
    cos1, sin1 = turn_of(turn_ref, 0)
    cos, sin = turn_of(turn_ref, lax.rem(mine + 2, blocks))
    height = ahead[0] - shrink * relaxed[0]
    zonal = ahead[1] - shrink * (cos1 * relaxed[1] + sin1 * relaxed[2])
    merid = ahead[2] - shrink * (cos1 * relaxed[2] - sin1 * relaxed[1])
    return height, cos * zonal - sin * merid, cos * merid + sin * zonal


def put_forcing(turn_ref, decay_ref, relaxed_ref, ahead_ref, term_ref, rows):
    lons = decay_ref.shape[1]
    per_plane = term_ref.shape[0] // 3
    for row in rows:
        for col in range(0, lons, LANES):
            where = (slice(row, row + 8), slice(col, col + LANES))
            relaxed = [relaxed_ref[(plane, *where)] for plane in range(3)]
            ahead = [ahead_ref[(plane, *where)] for plane in range(3)]
            at = row * lons // LANES + col * 8 // LANES
            for plane, term in enumerate(forcing(turn_ref, decay_ref[where], relaxed, ahead)):
                to = plane * per_plane + at
                term_ref[to : to + 8] = term


def relax_kernel(
    turn_ref, state_ref, second_ref, pair_ref, decay_ref, term_ref, relaxed_ref, ahead_ref, term, sem
):
    even = lax.rem(lax.axis_index("lat"), 2) == 0
    rows, lons = state_ref.shape[1:]
    state = []
    for plane in range(3):
        first = jnp.where(even, pair_ref[1, plane], pair_ref[0, plane])
        second = second_ref[plane]
        below = jnp.where(even, second, first)
        above = jnp.where(even, first, second)
        state.append(jnp.concatenate([below, state_ref[plane], above], axis=0))
    relaxed, ahead = two_blocks(state)
    per_plane = term.shape[0] // 3
    for row in range(0, rows, 8):
        for col in range(0, lons, LANES):
            cols = slice(col, col + LANES)
            at = row + HALO
            tiles = [[a[at : at + 8, cols] for a in state] for state in (relaxed, ahead)]
            to = row * lons // LANES + col * 8 // LANES
            for plane, value in enumerate(forcing(turn_ref, decay_ref[row : row + 8, cols], *tiles)):
                term[plane * per_plane + to : plane * per_plane + to + 8] = value
    copy = pltpu.make_async_copy(term, term_ref, sem.at[0])
    copy.start()
    for to, values in ((relaxed_ref, relaxed), (ahead_ref, ahead)):
        for plane, value in enumerate(values):
            to[plane] = value[HALO : HALO + rows]
    copy.wait()


def solve_kernel(places, decay_ref, term_ref, value_ref, values, sem):
    shrink = jnp.exp(-decay_ref[...])
    each = shrink.shape[0]
    parts = sem.shape[0]

    blocks = len(places)

    def at(slot):
        return slice(places[slot] * each, (places[slot] + 1) * each)

    value = term_ref[at(blocks - 1)]
    size = each * blocks // parts
    copies, done = [], set()
    for slot in range(blocks):
        if slot >= 2:
            value = shrink * value + term_ref[at(slot - 2)]
        values[at(slot)] = value
        done.add(places[slot] * parts // blocks)
        later = {place * parts // blocks for place in places[slot + 1 :]}
        for k in sorted(done - later):
            done.remove(k)
            part = pl.ds(k * size, size)
            copies.append(pltpu.make_async_copy(values.at[part], value_ref.at[part], sem.at[k]))
            copies[-1].start()
    for copy in copies:
        copy.wait()


def pass_kernel(blocks, both_ref, ahead_ref, passed_ref):
    mine = lax.axis_index("tm")
    odd = lax.rem(mine, 2) == 1
    last = mine == blocks - 2
    for plane in range(3):
        ahead, other = ahead_ref[plane], both_ref[1, plane]
        passed_ref[plane] = jnp.where(odd, ahead, jnp.where(last, other, ahead - other))


def residual_kernel(both_ref, got_ref, residual_ref):
    mine = lax.axis_index("tm")
    odd, first = lax.rem(mine, 2) == 1, mine == 0
    for plane in range(3):
        got = got_ref[plane]
        relaxed = jnp.where(odd, both_ref[0, plane], jnp.where(first, got, 0.0))
        residual_ref[0, plane] = got - relaxed


def finish_kernel(turn_ref, value_ref, got_ref, corrected_ref):
    mine = lax.axis_index("tm")
    first = mine == 0
    cos, sin = turn_of(turn_ref, mine)
    rows, lons = corrected_ref.shape[2:]
    per_plane = rows * lons // LANES
    at = 0
    for row in range(0, rows, 8):
        for col in range(0, lons, LANES):
            height, zonal, merid = (
                value_ref[plane * per_plane + at : plane * per_plane + at + 8] for plane in range(3)
            )
            values = (height, cos * zonal + sin * merid, cos * merid - sin * zonal)
            for plane in range(3):
                block = (plane, slice(row, row + 8), slice(col, col + LANES))
                corrected_ref[(0, *block)] = jnp.where(first, got_ref[block], values[plane])
            at += 8


def on_device(states, initial_state, coarse_decay):
    blocks, slabs = lax.axis_size("tm"), lax.axis_size("lat")
    mine, slab = lax.axis_index("tm"), lax.axis_index("lat")
    _, planes, rows, lons = states.shape
    size = planes * rows * lons
    each = size // LANES // blocks
    vmem = pl.BlockSpec(memory_space=pltpu.VMEM)
    hbm = pl.BlockSpec(memory_space=pltpu.HBM)
    f32 = functools.partial(jax.ShapeDtypeStruct, dtype=jnp.float32)
    whole, flat = f32((planes, rows, lons)), f32((size // LANES, LANES))
    params = pltpu.CompilerParams(vmem_limit_bytes=32 << 20)
    turn = jnp.asarray(turns(blocks))
    lead = 45 * blocks // 64
    order = [lead] + [block for block in range(blocks) if block != lead]
    places = [order.index(block) for block in range(blocks)]

    def exchanged(x):
        return lax.all_to_all(
            x.reshape(blocks, -1), "tm", 0, 0, axis_index_groups=[order], tiled=True
        ).reshape(-1, LANES)

    def long(steps):
        return pl.CostEstimate(flops=steps * size, bytes_accessed=8 * size, transcendentals=0)

    state = jnp.where(mine == blocks - 1, initial_state, states[0])
    even = slab % 2 == 0
    low, high = state[:, :HALO], state[:, -HALO:]
    outer = [(i, (i - 1 if i % 2 == 0 else i + 1) % slabs) for i in range(slabs)]
    second = lax.ppermute(jnp.where(even, low, high), "lat", outer)
    pairs = [[i, i + 1] for i in range(0, slabs, 2)]
    pair = lax.all_gather(jnp.where(even, high, low), "lat", axis_index_groups=pairs)

    tiles = coarse_decay.reshape(rows // 8, 8, lons // LANES, LANES).transpose(0, 2, 1, 3)
    tiles = tiles.reshape(-1, LANES)
    tiles = jnp.concatenate([tiles, tiles[:each]], axis=0)
    place = jnp.where(mine == lead, 0, jnp.where(mine < lead, mine + 1, mine))
    own_decay = lax.dynamic_slice_in_dim(tiles, lax.rem(place * each, rows * lons // LANES), each, 0)

    term, relaxed, ahead = pl.pallas_call(
        relax_kernel,
        out_shape=(flat, whole, whole),
        in_specs=[vmem] * 5,
        out_specs=(hbm, vmem, vmem),
        scratch_shapes=[pltpu.VMEM(flat.shape, jnp.float32), pltpu.SemaphoreType.DMA((1,))],
        compiler_params=params,
    )(turn, state, second, pair, coarse_decay)

    both = lax.all_gather(relaxed, "tm", axis_index_groups=[[i, i + 1] for i in range(0, blocks, 2)])
    passed = pl.pallas_call(
        functools.partial(pass_kernel, blocks),
        out_shape=whole,
        in_specs=[vmem, vmem],
        out_specs=vmem,
        compiler_params=params,
    )(both, ahead)
    got = lax.ppermute(passed, "tm", [(i, (i + 2) % blocks) for i in range(blocks)])
    residual = pl.pallas_call(
        residual_kernel,
        out_shape=f32((1, planes, rows, lons)),
        in_specs=[vmem, vmem],
        out_specs=vmem,
        compiler_params=params,
        cost_estimate=long(10**6),
    )(both, got)
    value = pl.pallas_call(
        functools.partial(solve_kernel, places),
        out_shape=flat,
        in_specs=[vmem, vmem],
        out_specs=hbm,
        scratch_shapes=[pltpu.VMEM(flat.shape, jnp.float32), pltpu.SemaphoreType.DMA((4,))],
        compiler_params=params,
    )(own_decay, exchanged(term))
    corrected = pl.pallas_call(
        finish_kernel,
        out_shape=f32((1, planes, rows, lons)),
        in_specs=[vmem] * 3,
        out_specs=vmem,
        compiler_params=params,
    )(turn, exchanged(value), got)
    return (corrected, residual)


def solution(mesh):
    placed = (P("tm", None, "lat", None), P(None, "lat", None), P("lat", None))
    return jax.shard_map(
        on_device,
        mesh=mesh,
        in_specs=placed,
        out_specs=(P("tm", None, "lat", None), P("tm", None, "lat", None)),
        check_vma=False,
    )
```

```python
import functools

import jax
import jax.numpy as jnp
import numpy as np
from jax import lax
from jax.experimental import pallas as pl
from jax.experimental.pallas import tpu as pltpu
from jax.sharding import PartitionSpec as P

STEPS = 4
TIME_STEP = 0.25
CORIOLIS = 0.3
TURN_ANGLE = 1.2
LANES = 128
HALO = 2 * STEPS


def turns(blocks):
    turn = complex(np.cos(np.float32(TURN_ANGLE)), np.sin(np.float32(TURN_ANGLE)))
    powers = np.cumprod(np.full(blocks, turn, np.complex128))
    return np.repeat(np.concatenate([powers.real, powers.imag])[:, None], LANES, 1).astype(np.float32)


def fine_step(height, zonal, merid):
    rows = height.shape[0]
    lons = height.shape[1]

    def sides(a):
        return (
            pltpu.roll(a, lons - 1, 1),
            pltpu.roll(a, 1, 1),
            pltpu.roll(a, rows - 1, 0),
            pltpu.roll(a, 1, 0),
        )

    he, hw, hn, hs = sides(height)
    ze, zw, zn, zs = sides(zonal)
    me, mw, mn, ms = sides(merid)
    half = 0.5 * TIME_STEP
    flux = ((1.0 + he) * ze - (1.0 + hw) * zw) + ((1.0 + hn) * mn - (1.0 + hs) * ms)
    new_height = 0.25 * ((he + hw) + (hn + hs)) - half * flux
    new_zonal = (
        0.25 * ((ze + zw) + (zn + zs))
        - half * (zonal * (ze - zw) + merid * (zn - zs) + (he - hw))
        + (TIME_STEP * CORIOLIS) * merid
    )
    new_merid = (
        0.25 * ((me + mw) + (mn + ms))
        - half * (zonal * (me - mw) + merid * (mn - ms) + (hn - hs))
        - (TIME_STEP * CORIOLIS) * zonal
    )
    return new_height, new_zonal, new_merid


def turn_of(turn_ref, slot):
    blocks = turn_ref.shape[0] // 2
    return turn_ref[pl.ds(slot, 1)], turn_ref[pl.ds(slot + blocks, 1)]


def two_blocks(state):
    for _ in range(STEPS):
        state = fine_step(*state)
    relaxed = state
    for _ in range(STEPS):
        state = fine_step(*state)
    return relaxed, state


def forcing(turn_ref, decay, relaxed, ahead):
    blocks = turn_ref.shape[0] // 2
    mine = lax.axis_index("tm")
    shrink = jnp.where(mine == blocks - 1, 0.0, jnp.exp(-decay))
    cos1, sin1 = turn_of(turn_ref, 0)
    cos, sin = turn_of(turn_ref, lax.rem(mine + 2, blocks))
    height = ahead[0] - shrink * relaxed[0]
    zonal = ahead[1] - shrink * (cos1 * relaxed[1] + sin1 * relaxed[2])
    merid = ahead[2] - shrink * (cos1 * relaxed[2] - sin1 * relaxed[1])
    return height, cos * zonal - sin * merid, cos * merid + sin * zonal


def put_forcing(turn_ref, decay_ref, relaxed_ref, ahead_ref, term_ref, rows):
    lons = decay_ref.shape[1]
    per_plane = term_ref.shape[0] // 3
    for row in rows:
        for col in range(0, lons, LANES):
            where = (slice(row, row + 8), slice(col, col + LANES))
            relaxed = [relaxed_ref[(plane, *where)] for plane in range(3)]
            ahead = [ahead_ref[(plane, *where)] for plane in range(3)]
            at = row * lons // LANES + col * 8 // LANES
            for plane, term in enumerate(forcing(turn_ref, decay_ref[where], relaxed, ahead)):
                to = plane * per_plane + at
                term_ref[to : to + 8] = term


def relax_kernel(
    turn_ref, state_ref, first_ref, pair_ref, decay_ref, term_ref, relaxed_ref, ahead_ref, term, sem
):
    even = lax.rem(lax.axis_index("lat"), 2) == 0
    rows, lons = state_ref.shape[1:]
    state = []
    for plane in range(3):
        first = first_ref[plane]
        second = jnp.where(even, pair_ref[0, plane], pair_ref[1, plane])
        below = jnp.where(even, second, first)
        above = jnp.where(even, first, second)
        state.append(jnp.concatenate([below, state_ref[plane], above], axis=0))
    relaxed, ahead = two_blocks(state)
    per_plane = term.shape[0] // 3
    for row in range(0, rows, 8):
        for col in range(0, lons, LANES):
            cols = slice(col, col + LANES)
            at = row + HALO
            tiles = [[a[at : at + 8, cols] for a in state] for state in (relaxed, ahead)]
            to = row * lons // LANES + col * 8 // LANES
            for plane, value in enumerate(forcing(turn_ref, decay_ref[row : row + 8, cols], *tiles)):
                term[plane * per_plane + to : plane * per_plane + to + 8] = value
    copy = pltpu.make_async_copy(term, term_ref, sem.at[0])
    copy.start()
    for to, values in ((relaxed_ref, relaxed), (ahead_ref, ahead)):
        for plane, value in enumerate(values):
            to[plane] = value[HALO : HALO + rows]
    copy.wait()


def solve_kernel(places, decay_ref, term_ref, value_ref, values, sem):
    shrink = jnp.exp(-decay_ref[...])
    each = shrink.shape[0]
    parts = sem.shape[0]

    blocks = len(places)

    def at(slot):
        return slice(places[slot] * each, (places[slot] + 1) * each)

    value = term_ref[at(blocks - 1)]
    size = each * blocks // parts
    copies, done = [], set()
    for slot in range(blocks):
        if slot >= 2:
            value = shrink * value + term_ref[at(slot - 2)]
        values[at(slot)] = value
        done.add(places[slot] * parts // blocks)
        later = {place * parts // blocks for place in places[slot + 1 :]}
        for k in sorted(done - later):
            done.remove(k)
            part = pl.ds(k * size, size)
            copies.append(pltpu.make_async_copy(values.at[part], value_ref.at[part], sem.at[k]))
            copies[-1].start()
    for copy in copies:
        copy.wait()


def pass_kernel(blocks, both_ref, ahead_ref, passed_ref):
    mine = lax.axis_index("tm")
    odd = lax.rem(mine, 2) == 1
    last = mine == blocks - 2
    for plane in range(3):
        ahead, other = ahead_ref[plane], both_ref[1, plane]
        passed_ref[plane] = jnp.where(odd, ahead, jnp.where(last, other, ahead - other))


def residual_kernel(both_ref, got_ref, residual_ref):
    mine = lax.axis_index("tm")
    odd, first = lax.rem(mine, 2) == 1, mine == 0
    for plane in range(3):
        got = got_ref[plane]
        relaxed = jnp.where(odd, both_ref[0, plane], jnp.where(first, got, 0.0))
        residual_ref[0, plane] = got - relaxed


def finish_kernel(turn_ref, value_ref, got_ref, corrected_ref):
    mine = lax.axis_index("tm")
    first = mine == 0
    cos, sin = turn_of(turn_ref, mine)
    rows, lons = corrected_ref.shape[2:]
    per_plane = rows * lons // LANES
    at = 0
    for row in range(0, rows, 8):
        for col in range(0, lons, LANES):
            height, zonal, merid = (
                value_ref[plane * per_plane + at : plane * per_plane + at + 8] for plane in range(3)
            )
            values = (height, cos * zonal + sin * merid, cos * merid - sin * zonal)
            for plane in range(3):
                block = (plane, slice(row, row + 8), slice(col, col + LANES))
                corrected_ref[(0, *block)] = jnp.where(first, got_ref[block], values[plane])
            at += 8


def on_device(states, initial_state, coarse_decay):
    blocks, slabs = lax.axis_size("tm"), lax.axis_size("lat")
    mine, slab = lax.axis_index("tm"), lax.axis_index("lat")
    _, planes, rows, lons = states.shape
    size = planes * rows * lons
    each = size // LANES // blocks
    vmem = pl.BlockSpec(memory_space=pltpu.VMEM)
    hbm = pl.BlockSpec(memory_space=pltpu.HBM)
    f32 = functools.partial(jax.ShapeDtypeStruct, dtype=jnp.float32)
    whole, flat = f32((planes, rows, lons)), f32((size // LANES, LANES))
    params = pltpu.CompilerParams(vmem_limit_bytes=32 << 20)
    turn = jnp.asarray(turns(blocks))
    lead = 45 * blocks // 64
    order = [lead] + [block for block in range(blocks) if block != lead]
    places = [order.index(block) for block in range(blocks)]

    def exchanged(x):
        return lax.all_to_all(
            x.reshape(blocks, -1), "tm", 0, 0, axis_index_groups=[order], tiled=True
        ).reshape(-1, LANES)

    def long(steps):
        return pl.CostEstimate(flops=steps * size, bytes_accessed=8 * size, transcendentals=0)

    state = jnp.where(mine == blocks - 1, initial_state, states[0])
    even = slab % 2 == 0
    low, high = state[:, :HALO], state[:, -HALO:]
    inner = [(i, i ^ 1) for i in range(slabs)]
    first = lax.ppermute(jnp.where(even, high, low), "lat", inner)
    pairs = [[i, (i + 1) % slabs] for i in range(1, slabs, 2)]
    pair = lax.all_gather(jnp.where(even, low, high), "lat", axis_index_groups=pairs)

    tiles = coarse_decay.reshape(rows // 8, 8, lons // LANES, LANES).transpose(0, 2, 1, 3)
    tiles = tiles.reshape(-1, LANES)
    tiles = jnp.concatenate([tiles, tiles[:each]], axis=0)
    place = jnp.where(mine == lead, 0, jnp.where(mine < lead, mine + 1, mine))
    own_decay = lax.dynamic_slice_in_dim(tiles, lax.rem(place * each, rows * lons // LANES), each, 0)

    term, relaxed, ahead = pl.pallas_call(
        relax_kernel,
        out_shape=(flat, whole, whole),
        in_specs=[vmem] * 5,
        out_specs=(hbm, vmem, vmem),
        scratch_shapes=[pltpu.VMEM(flat.shape, jnp.float32), pltpu.SemaphoreType.DMA((1,))],
        compiler_params=params,
    )(turn, state, first, pair, coarse_decay)

    both = lax.all_gather(relaxed, "tm", axis_index_groups=[[i, i + 1] for i in range(0, blocks, 2)])
    passed = pl.pallas_call(
        functools.partial(pass_kernel, blocks),
        out_shape=whole,
        in_specs=[vmem, vmem],
        out_specs=vmem,
        compiler_params=params,
    )(both, ahead)
    got = lax.ppermute(passed, "tm", [(i, (i + 2) % blocks) for i in range(blocks)])
    residual = pl.pallas_call(
        residual_kernel,
        out_shape=f32((1, planes, rows, lons)),
        in_specs=[vmem, vmem],
        out_specs=vmem,
        compiler_params=params,
        cost_estimate=long(10**6),
    )(both, got)
    value = pl.pallas_call(
        functools.partial(solve_kernel, places),
        out_shape=flat,
        in_specs=[vmem, vmem],
        out_specs=hbm,
        scratch_shapes=[pltpu.VMEM(flat.shape, jnp.float32), pltpu.SemaphoreType.DMA((4,))],
        compiler_params=params,
    )(own_decay, exchanged(term))
    corrected = pl.pallas_call(
        finish_kernel,
        out_shape=f32((1, planes, rows, lons)),
        in_specs=[vmem] * 3,
        out_specs=vmem,
        compiler_params=params,
    )(turn, exchanged(value), got)
    return (corrected, residual)


def solution(mesh):
    placed = (P("tm", None, "lat", None), P(None, "lat", None), P("lat", None))
    return jax.shard_map(
        on_device,
        mesh=mesh,
        in_specs=placed,
        out_specs=(P("tm", None, "lat", None), P("tm", None, "lat", None)),
        check_vma=False,
    )
```

```python
import functools

import jax
import jax.numpy as jnp
import numpy as np
from jax import lax
from jax.experimental import pallas as pl
from jax.experimental.pallas import tpu as pltpu
from jax.sharding import PartitionSpec as P

STEPS = 4
TIME_STEP = 0.25
CORIOLIS = 0.3
TURN_ANGLE = 1.2
LANES = 128
HALO = 2 * STEPS


def turns(blocks):
    turn = complex(np.cos(np.float32(TURN_ANGLE)), np.sin(np.float32(TURN_ANGLE)))
    powers = np.cumprod(np.full(blocks, turn, np.complex128))
    return np.repeat(np.concatenate([powers.real, powers.imag])[:, None], LANES, 1).astype(np.float32)


def fine_step(height, zonal, merid):
    rows = height.shape[0]
    lons = height.shape[1]

    def sides(a):
        return (
            pltpu.roll(a, lons - 1, 1),
            pltpu.roll(a, 1, 1),
            pltpu.roll(a, rows - 1, 0),
            pltpu.roll(a, 1, 0),
        )

    he, hw, hn, hs = sides(height)
    ze, zw, zn, zs = sides(zonal)
    me, mw, mn, ms = sides(merid)
    half = 0.5 * TIME_STEP
    flux = ((1.0 + he) * ze - (1.0 + hw) * zw) + ((1.0 + hn) * mn - (1.0 + hs) * ms)
    new_height = 0.25 * ((he + hw) + (hn + hs)) - half * flux
    new_zonal = (
        0.25 * ((ze + zw) + (zn + zs))
        - half * (zonal * (ze - zw) + merid * (zn - zs) + (he - hw))
        + (TIME_STEP * CORIOLIS) * merid
    )
    new_merid = (
        0.25 * ((me + mw) + (mn + ms))
        - half * (zonal * (me - mw) + merid * (mn - ms) + (hn - hs))
        - (TIME_STEP * CORIOLIS) * zonal
    )
    return new_height, new_zonal, new_merid


def turn_of(turn_ref, slot):
    blocks = turn_ref.shape[0] // 2
    return turn_ref[pl.ds(slot, 1)], turn_ref[pl.ds(slot + blocks, 1)]


def two_blocks(state):
    for _ in range(STEPS):
        state = fine_step(*state)
    relaxed = state
    for _ in range(STEPS):
        state = fine_step(*state)
    return relaxed, state


def forcing(turn_ref, decay, relaxed, ahead):
    blocks = turn_ref.shape[0] // 2
    mine = lax.axis_index("tm")
    shrink = jnp.where(mine == blocks - 1, 0.0, jnp.exp(-decay))
    cos1, sin1 = turn_of(turn_ref, 0)
    cos, sin = turn_of(turn_ref, lax.rem(mine + 2, blocks))
    height = ahead[0] - shrink * relaxed[0]
    zonal = ahead[1] - shrink * (cos1 * relaxed[1] + sin1 * relaxed[2])
    merid = ahead[2] - shrink * (cos1 * relaxed[2] - sin1 * relaxed[1])
    return height, cos * zonal - sin * merid, cos * merid + sin * zonal


def put_forcing(turn_ref, decay_ref, relaxed_ref, ahead_ref, term_ref, rows):
    lons = decay_ref.shape[1]
    per_plane = term_ref.shape[0] // 3
    for row in rows:
        for col in range(0, lons, LANES):
            where = (slice(row, row + 8), slice(col, col + LANES))
            relaxed = [relaxed_ref[(plane, *where)] for plane in range(3)]
            ahead = [ahead_ref[(plane, *where)] for plane in range(3)]
            at = row * lons // LANES + col * 8 // LANES
            for plane, term in enumerate(forcing(turn_ref, decay_ref[where], relaxed, ahead)):
                to = plane * per_plane + at
                term_ref[to : to + 8] = term


def relax_kernel(
    turn_ref, state_ref, first_ref, pair_ref, decay_ref, term_ref, relaxed_ref, ahead_ref, term, sem
):
    even = lax.rem(lax.axis_index("lat"), 2) == 0
    rows, lons = state_ref.shape[1:]
    state = []
    for plane in range(3):
        first = first_ref[plane]
        second = jnp.where(even, pair_ref[0, plane], pair_ref[1, plane])
        below = jnp.where(even, second, first)
        above = jnp.where(even, first, second)
        state.append(jnp.concatenate([below, state_ref[plane], above], axis=0))
    relaxed, ahead = two_blocks(state)
    per_plane = term.shape[0] // 3
    copies = []
    for row in range(0, rows, 8):
        for col in range(0, lons, LANES):
            cols = slice(col, col + LANES)
            at = row + HALO
            tiles = [[a[at : at + 8, cols] for a in state] for state in (relaxed, ahead)]
            to = row * lons // LANES + col * 8 // LANES
            for plane, value in enumerate(forcing(turn_ref, decay_ref[row : row + 8, cols], *tiles)):
                term[plane * per_plane + to : plane * per_plane + to + 8] = value
        if (row + 8) % (rows // 2) == 0:
            half = per_plane // 2
            for plane in range(3):
                part = pl.ds(plane * per_plane + (row + 8) * lons // LANES - half, half)
                copies.append(
                    pltpu.make_async_copy(term.at[part], term_ref.at[part], sem.at[len(copies)])
                )
                copies[-1].start()
    for to, values in ((relaxed_ref, relaxed), (ahead_ref, ahead)):
        for plane, value in enumerate(values):
            to[plane] = value[HALO : HALO + rows]
    for copy in copies:
        copy.wait()


def solve_kernel(places, decay_ref, term_ref, value_ref, values, sem):
    shrink = jnp.exp(-decay_ref[...])
    each = shrink.shape[0]
    parts = sem.shape[0]

    blocks = len(places)

    def at(slot):
        return slice(places[slot] * each, (places[slot] + 1) * each)

    value = term_ref[at(blocks - 1)]
    size = each * blocks // parts
    copies, done = [], set()
    for slot in range(blocks):
        if slot >= 2:
            value = shrink * value + term_ref[at(slot - 2)]
        values[at(slot)] = value
        done.add(places[slot] * parts // blocks)
        later = {place * parts // blocks for place in places[slot + 1 :]}
        for k in sorted(done - later):
            done.remove(k)
            part = pl.ds(k * size, size)
            copies.append(pltpu.make_async_copy(values.at[part], value_ref.at[part], sem.at[k]))
            copies[-1].start()
    for copy in copies:
        copy.wait()


def pass_kernel(blocks, both_ref, ahead_ref, passed_ref):
    mine = lax.axis_index("tm")
    odd = lax.rem(mine, 2) == 1
    last = mine == blocks - 2
    for plane in range(3):
        ahead, other = ahead_ref[plane], both_ref[1, plane]
        passed_ref[plane] = jnp.where(odd, ahead, jnp.where(last, other, ahead - other))


def residual_kernel(both_ref, got_ref, residual_ref):
    mine = lax.axis_index("tm")
    odd, first = lax.rem(mine, 2) == 1, mine == 0
    for plane in range(3):
        got = got_ref[plane]
        relaxed = jnp.where(odd, both_ref[0, plane], jnp.where(first, got, 0.0))
        residual_ref[0, plane] = got - relaxed


def finish_kernel(turn_ref, value_ref, got_ref, corrected_ref):
    mine = lax.axis_index("tm")
    first = mine == 0
    cos, sin = turn_of(turn_ref, mine)
    rows, lons = corrected_ref.shape[2:]
    per_plane = rows * lons // LANES
    at = 0
    for row in range(0, rows, 8):
        for col in range(0, lons, LANES):
            height, zonal, merid = (
                value_ref[plane * per_plane + at : plane * per_plane + at + 8] for plane in range(3)
            )
            values = (height, cos * zonal + sin * merid, cos * merid - sin * zonal)
            for plane in range(3):
                block = (plane, slice(row, row + 8), slice(col, col + LANES))
                corrected_ref[(0, *block)] = jnp.where(first, got_ref[block], values[plane])
            at += 8


def on_device(states, initial_state, coarse_decay):
    blocks, slabs = lax.axis_size("tm"), lax.axis_size("lat")
    mine, slab = lax.axis_index("tm"), lax.axis_index("lat")
    _, planes, rows, lons = states.shape
    size = planes * rows * lons
    each = size // LANES // blocks
    vmem = pl.BlockSpec(memory_space=pltpu.VMEM)
    hbm = pl.BlockSpec(memory_space=pltpu.HBM)
    f32 = functools.partial(jax.ShapeDtypeStruct, dtype=jnp.float32)
    whole, flat = f32((planes, rows, lons)), f32((size // LANES, LANES))
    params = pltpu.CompilerParams(vmem_limit_bytes=32 << 20)
    turn = jnp.asarray(turns(blocks))
    lead = 45 * blocks // 64
    order = [lead] + [block for block in range(blocks) if block != lead]
    places = [order.index(block) for block in range(blocks)]

    def exchanged(x):
        return lax.all_to_all(
            x.reshape(blocks, -1), "tm", 0, 0, axis_index_groups=[order], tiled=True
        ).reshape(-1, LANES)

    def long(steps):
        return pl.CostEstimate(flops=steps * size, bytes_accessed=8 * size, transcendentals=0)

    state = jnp.where(mine == blocks - 1, initial_state, states[0])
    even = slab % 2 == 0
    low, high = state[:, :HALO], state[:, -HALO:]
    inner = [(i, i ^ 1) for i in range(slabs)]
    first = lax.ppermute(jnp.where(even, high, low), "lat", inner)
    pairs = [[i, (i + 1) % slabs] for i in range(1, slabs, 2)]
    pair = lax.all_gather(jnp.where(even, low, high), "lat", axis_index_groups=pairs)

    tiles = coarse_decay.reshape(rows // 8, 8, lons // LANES, LANES).transpose(0, 2, 1, 3)
    tiles = tiles.reshape(-1, LANES)
    tiles = jnp.concatenate([tiles, tiles[:each]], axis=0)
    place = jnp.where(mine == lead, 0, jnp.where(mine < lead, mine + 1, mine))
    own_decay = lax.dynamic_slice_in_dim(tiles, lax.rem(place * each, rows * lons // LANES), each, 0)

    term, relaxed, ahead = pl.pallas_call(
        relax_kernel,
        out_shape=(flat, whole, whole),
        in_specs=[vmem] * 5,
        out_specs=(hbm, vmem, vmem),
        scratch_shapes=[pltpu.VMEM(flat.shape, jnp.float32), pltpu.SemaphoreType.DMA((6,))],
        compiler_params=params,
    )(turn, state, first, pair, coarse_decay)

    both = lax.all_gather(relaxed, "tm", axis_index_groups=[[i, i + 1] for i in range(0, blocks, 2)])
    passed = pl.pallas_call(
        functools.partial(pass_kernel, blocks),
        out_shape=whole,
        in_specs=[vmem, vmem],
        out_specs=vmem,
        compiler_params=params,
    )(both, ahead)
    got = lax.ppermute(passed, "tm", [(i, (i + 2) % blocks) for i in range(blocks)])
    residual = pl.pallas_call(
        residual_kernel,
        out_shape=f32((1, planes, rows, lons)),
        in_specs=[vmem, vmem],
        out_specs=vmem,
        compiler_params=params,
        cost_estimate=long(10**6),
    )(both, got)
    value = pl.pallas_call(
        functools.partial(solve_kernel, places),
        out_shape=flat,
        in_specs=[vmem, vmem],
        out_specs=hbm,
        scratch_shapes=[pltpu.VMEM(flat.shape, jnp.float32), pltpu.SemaphoreType.DMA((4,))],
        compiler_params=params,
    )(own_decay, exchanged(term))
    corrected = pl.pallas_call(
        finish_kernel,
        out_shape=f32((1, planes, rows, lons)),
        in_specs=[vmem] * 3,
        out_specs=vmem,
        compiler_params=params,
    )(turn, exchanged(value), got)
    return (corrected, residual)


def solution(mesh):
    placed = (P("tm", None, "lat", None), P(None, "lat", None), P("lat", None))
    return jax.shard_map(
        on_device,
        mesh=mesh,
        in_specs=placed,
        out_specs=(P("tm", None, "lat", None), P("tm", None, "lat", None)),
        check_vma=False,
    )
```
